32 devices in a mesh: ctx: 8 (over z, y), head: 4 (over x, core).
Axes of the slice: x: 2, y: 2, z: 4, core: 2. Of those that a mesh axis runs over, the one named last changes fastest.
Arguments:
- activations: bfloat16 [4096, 2048], P(('ctx', 'head')), may hold values from -6 to 6
- w_in: bfloat16 [2048, 14336], P('ctx', 'head'), may hold values from -0.125 to 0.125
- w_beta: bfloat16 [2048, 48], P('ctx', 'head'), may hold values from -0.0625 to 0.0625
- beta_bias: float32 [48], P('head'), may hold values from -2 to 10
- head_gain: float32 [2048], P('head'), may hold values from 0.1 to 1.9
- w_out: bfloat16 [2048, 2048], P('head'), may hold values from -0.125 to 0.125
Outputs:
- mixed_out: bfloat16 [4096, 2048], P(('ctx', 'head'))
The draws below stay inside these ranges and needn't reach their ends.
All inputs are finite; a program needn't handle non-finite values.
Results may differ from the reference program's by a relative error of at most 0.015.
The reference program's roundings to bfloat16 on the way count: a program that leaves them out, or rounds other values in their place, can miss the bound.
Values may be sent and summed in bfloat16 or wider, within the bound.
A program may use at most 128 MiB of HBM per device.

```python
import jax
import jax.numpy as jnp
from jax import lax

D = 2048
H = 16
DK = 128
NF = 3
BLOCK = 64
HEADS_DEV = 4
TOKENS = 4096


def draw_beta_bias(key, part):
    key = jax.random.fold_in(key, 7)
    order_key, slow_key, fast_key = jax.random.split(key, 3)
    slow_count = H // 2
    fast_edge = 1.5
    ranking = jax.random.permutation(order_key, H)
    slow_heads = ranking < slow_count
    slow_level = jax.random.uniform(slow_key, (H, NF), jnp.float32, 8.0, 10.0)
    fast_level = jax.random.uniform(fast_key, (H, NF), jnp.float32, -fast_edge, fast_edge)
    return jnp.where(slow_heads[:, None], slow_level, fast_level).reshape(H * NF)


def steps_of(rng, extent, cuts, smallest, top_value):
    level, own = 1.0, jax.random.fold_in(rng, 6)
    for position, blocks in cuts:
        steps = jnp.exp(jax.random.uniform(jax.random.fold_in(own, position), (blocks,), jnp.float32, smallest / len(cuts), top_value / len(cuts)))
        level = level * jnp.repeat(steps, extent[position] // blocks).reshape([-1 if axis == position else 1 for axis in range(len(extent))])
    return level


def bell_draw(stream_key, shape, deviation, most, cuts=(), held_as=jnp.bfloat16):
    gain = steps_of(stream_key, shape, cuts, -0.22, 0.18) if cuts else 1.0
    array = jax.random.normal(stream_key, shape, jnp.float32) * deviation * gain
    return jnp.minimum(jnp.maximum(array, -most), most).astype(held_as)


def setup_inputs(seed: int = 0) -> dict:
    keys = jax.random.split(jax.random.key(seed), 7)
    activations = bell_draw(keys[0], (TOKENS, D), 1.0, 6.0, ((0, 32),))
    w_in = bell_draw(keys[1], (D, H * (1 + 2 * NF) * DK), D ** -0.5, 0.125, ((0, 8), (1, 4)))
    w_beta = bell_draw(keys[2], (D, H * NF), (4 * D) ** -0.5, 0.0625, ((0, 8), (1, 4)))
    beta_bias = draw_beta_bias(jax.random.fold_in(keys[6], 71), 0)
    head_gain = jnp.clip(1.0 + 0.18 * jax.random.normal(keys[4], (H * DK,), jnp.float32), 0.1, 1.9)
    w_out = bell_draw(keys[5], (H * DK, D), (H * DK) ** -0.5, 0.125, ((0, 4),))
    return {"activations": activations, "w_in": w_in, "w_beta": w_beta, "beta_bias": beta_bias, "head_gain": head_gain, "w_out": w_out}


EPSILON = 1e-06
PRECISE = lax.Precision.HIGHEST

def matmul(form, left, right):
    return jnp.einsum(form, left, right, precision=PRECISE)

def block_terms(unit_keys, values, beta_rows):
    gram_mat = matmul('...id,...jd->...ij', unit_keys, unit_keys)
    length = unit_keys.shape[-2]
    strict = jnp.tril(jnp.ones((length, length), jnp.float32), -1)
    system = jnp.eye(length, dtype=jnp.float32) + strict * beta_rows[..., :, None] * gram_mat
    right_side = jnp.concatenate([beta_rows[..., None] * unit_keys, beta_rows[..., None] * values], axis=-1)
    solved = jax.scipy.linalg.solve_triangular(system, right_side, lower=True, unit_diagonal=True)
    split_at = unit_keys.shape[-1]
    return (solved[..., :split_at], solved[..., split_at:])

def head_outputs(activations, w_head, beta_head, bias_head, gain_head):
    projected = jnp.dot(activations.astype(jnp.float32), w_head.astype(jnp.float32), preferred_element_type=jnp.float32).astype(jnp.bfloat16)
    projected = lax.optimization_barrier(projected).astype(jnp.float32)
    logits = jnp.dot(activations.astype(jnp.float32), beta_head.astype(jnp.float32), preferred_element_type=jnp.float32) + bias_head
    beta_rows = 2.0 / (1.0 + jnp.exp(-logits))
    pieces = projected.reshape(TOKENS, 1 + 2 * NF, DK)
    queries = pieces[:, 0]
    raw_keys = pieces[:, 1:1 + NF]
    unit_keys = raw_keys / jnp.sqrt(lax.optimization_barrier(jnp.sum(raw_keys * raw_keys, axis=-1, keepdims=True)) + EPSILON)
    values = pieces[:, 1 + NF:]
    nblocks = TOKENS // BLOCK
    factor_len = BLOCK * NF
    unit_keys = unit_keys.reshape(nblocks, factor_len, DK)
    values = values.reshape(nblocks, factor_len, DK)
    beta_rows = beta_rows.reshape(nblocks, factor_len)
    queries = queries.reshape(nblocks, BLOCK, DK)
    w_rows, u_rows = block_terms(unit_keys, values, beta_rows)
    causal = (jnp.arange(factor_len)[None, :] <= NF * jnp.arange(BLOCK)[:, None] + NF - 1).astype(jnp.float32)

    def advance(carried, blockwise):
        query_blk, key_blk, w_blk, u_blk = blockwise
        scores = matmul('id,jd->ij', query_blk, key_blk) * causal
        fresh_rows = u_blk - matmul('jd,ed->je', w_blk, carried)
        emitted = matmul('id,ed->ie', query_blk, carried) + matmul('ij,je->ie', scores, fresh_rows)
        carried = carried + matmul('je,jd->ed', fresh_rows, key_blk)
        return (carried, emitted)
    ignored, attended = lax.scan(advance, jnp.zeros((DK, DK), jnp.float32), (queries, unit_keys, w_rows, u_rows))
    attended = attended.reshape(TOKENS, DK)
    scale = 1.0 / jnp.sqrt(lax.optimization_barrier(jnp.mean(attended * attended, axis=-1, keepdims=True)) + EPSILON)
    return (attended * scale * gain_head).astype(jnp.bfloat16)

def reference(activations, w_in, w_beta, beta_bias, head_gain, w_out):
    col_width = (1 + 2 * NF) * DK

    def one_head(head_index):
        w_head = lax.dynamic_slice_in_dim(w_in, head_index * col_width, col_width, 1)
        beta_head = lax.dynamic_slice_in_dim(w_beta, head_index * NF, NF, 1)
        bias_head = lax.dynamic_slice_in_dim(beta_bias, head_index * NF, NF, 0)
        gain_head = lax.dynamic_slice_in_dim(head_gain, head_index * DK, DK, 0)
        return head_outputs(activations, w_head, beta_head, bias_head, gain_head)
    normed = lax.map(one_head, jnp.arange(H, dtype=jnp.int32))
    summed = jnp.zeros((TOKENS, D), jnp.float32)
    for group_index in range(H // HEADS_DEV):
        selected = normed[group_index * HEADS_DEV:(group_index + 1) * HEADS_DEV]
        selected = jnp.transpose(selected, (1, 0, 2)).reshape(TOKENS, HEADS_DEV * DK)
        w_rows = w_out[group_index * HEADS_DEV * DK:(group_index + 1) * HEADS_DEV * DK]
        partial_value = jnp.dot(selected.astype(jnp.float32), w_rows.astype(jnp.float32), preferred_element_type=jnp.float32).astype(jnp.bfloat16)
        summed = summed + lax.optimization_barrier(partial_value).astype(jnp.float32)
    return summed.astype(jnp.bfloat16)
```

```python
import functools

import jax
import jax.numpy as jnp
from jax import lax
from jax.experimental import pallas as pl
from jax.experimental.pallas import tpu as pltpu
from jax.sharding import PartitionSpec as P

DK = 128
NF = 3
BLOCK = 64
HEADS_DEV = 4
FACTORS = BLOCK * NF
COLS = (1 + 2 * NF) * DK
EPSILON = 1e-06
PRECISE = lax.Precision.HIGHEST
MESH = pl.DeviceIdType.MESH
BF16 = jnp.bfloat16
F32 = jnp.float32


def gather_kernel(ctx_n, head_n, heads, w_in, w_beta, acts, w_out, w_all, beta_all, acts_all, out_all,
                  local_sem, w_send, w_recv, b_send, b_recv, a_send, a_recv, o_send, o_recv):
    ctx, head = lax.axis_index("ctx"), lax.axis_index("head")
    place = lax.rem(ctx, heads)
    base = ctx - place
    team = [(dc, dg) for dc in range(heads) for dg in range(head_n) if (dc, dg) != (0, 0)]

    def teammate(dc, dg):
        return (base + lax.rem(place + dc, heads), lax.rem(head + dg, head_n))

    barrier = pltpu.get_barrier_semaphore()
    for off in range(1, ctx_n):
        pl.semaphore_signal(barrier, inc=1, device_id=(lax.rem(ctx + off, ctx_n), head), device_id_type=MESH)
    for dc, dg in team:
        pl.semaphore_signal(barrier, inc=1, device_id=teammate(dc, dg), device_id_type=MESH)
    pl.semaphore_wait(barrier, ctx_n - 1 + len(team))

    def columns(of):
        return w_in.at[:, pl.ds(pl.multiple_of(lax.rem(of, heads) * COLS, DK), COLS)]

    copies = []

    def send(src, dst, ssem, rsem, device):
        copy = pltpu.make_async_remote_copy(src_ref=src, dst_ref=dst, send_sem=ssem, recv_sem=rsem,
                                            device_id=device, device_id_type=MESH)
        copy.start()
        copies.append(copy)

    order = sorted(range(1, ctx_n), key=lambda off: -min(off, ctx_n - off))
    for off in order:
        to = lax.rem(ctx + off, ctx_n)
        send(columns(to), w_all.at[ctx], w_send.at[off], w_recv.at[off], (to, head))
        send(w_beta, beta_all.at[ctx], b_send.at[off], b_recv.at[off], (to, head))
    for n, (dc, dg) in enumerate(team):
        send(acts, acts_all.at[place * head_n + head], a_send.at[n], a_recv.at[n], teammate(dc, dg))
    for off in range(1, head_n):
        send(w_out, out_all.at[head], o_send.at[off], o_recv.at[off], (ctx, lax.rem(head + off, head_n)))
    own = [
        pltpu.make_async_copy(columns(ctx), w_all.at[ctx], local_sem.at[0]),
        pltpu.make_async_copy(w_beta, beta_all.at[ctx], local_sem.at[1]),
        pltpu.make_async_copy(acts, acts_all.at[place * head_n + head], local_sem.at[2]),
        pltpu.make_async_copy(w_out, out_all.at[head], local_sem.at[3]),
    ]
    for copy in own:
        copy.start()
    for copy in own + copies:
        copy.wait()


def gather_all(ctx_n, head_n, heads, w_in, w_beta, acts, w_out):
    team = heads * head_n
    sems = [pltpu.SemaphoreType.DMA((n,)) for n in (4, ctx_n, ctx_n, ctx_n, ctx_n, team, team, head_n, head_n)]
    return pl.pallas_call(
        functools.partial(gather_kernel, ctx_n, head_n, heads),
        out_shape=(
            jax.ShapeDtypeStruct((ctx_n, w_in.shape[0], COLS), BF16),
            jax.ShapeDtypeStruct((ctx_n,) + w_beta.shape, BF16),
            jax.ShapeDtypeStruct((team,) + acts.shape, BF16),
            jax.ShapeDtypeStruct((head_n,) + w_out.shape, BF16),
        ),
        in_specs=[pl.BlockSpec(memory_space=pl.ANY)] * 4,
        out_specs=(pl.BlockSpec(memory_space=pl.ANY),) * 4,
        scratch_shapes=sems,
        compiler_params=pltpu.CompilerParams(collective_id=0, has_side_effects=True),
    )(w_in, w_beta, acts, w_out)


def exchange_kernel(head_n, heads, rows, mine, got, local_sem, send_sem, recv_sem):
    ctx, head = lax.axis_index("ctx"), lax.axis_index("head")
    place = lax.rem(ctx, heads)
    base = ctx - place
    team = [(dc, dg) for dc in range(heads) for dg in range(head_n) if (dc, dg) != (0, 0)]
    barrier = pltpu.get_barrier_semaphore()
    for dc, dg in team:
        device = (base + lax.rem(place + dc, heads), lax.rem(head + dg, head_n))
        pl.semaphore_signal(barrier, inc=1, device_id=device, device_id_type=MESH)
    pl.semaphore_wait(barrier, len(team))
    own_slot = head * heads + place

    def tokens_of(to_place, to_head):
        return mine.at[pl.ds(pl.multiple_of((to_place * head_n + to_head) * rows, rows), rows), :]

    copies = []
    for n, (dc, dg) in enumerate(team):
        to_place, to_head = lax.rem(place + dc, heads), lax.rem(head + dg, head_n)
        copy = pltpu.make_async_remote_copy(
            src_ref=tokens_of(to_place, to_head), dst_ref=got.at[own_slot], send_sem=send_sem.at[n],
            recv_sem=recv_sem.at[n], device_id=(base + to_place, to_head), device_id_type=MESH)
        copy.start()
        copies.append(copy)
    own = pltpu.make_async_copy(tokens_of(place, head), got.at[own_slot], local_sem)
    own.start()
    for copy in [own] + copies:
        copy.wait()


def exchange(head_n, heads, rows, normed):
    team = heads * head_n
    return pl.pallas_call(
        functools.partial(exchange_kernel, head_n, heads, rows),
        out_shape=jax.ShapeDtypeStruct((team, rows, DK), BF16),
        in_specs=[pl.BlockSpec(memory_space=pltpu.VMEM)],
        out_specs=pl.BlockSpec(memory_space=pltpu.VMEM),
        scratch_shapes=[pltpu.SemaphoreType.DMA, pltpu.SemaphoreType.DMA((team,)), pltpu.SemaphoreType.DMA((team,))],
        compiler_params=pltpu.CompilerParams(collective_id=1, has_side_effects=True),
    )(normed)


def halves(x):
    top = x.astype(BF16)
    return top, (x - top.astype(F32)).astype(BF16)


def dot(a, b, dims):
    return lax.dot_general(a, b, (dims, ((), ())), preferred_element_type=F32)


NN = ((1,), (0,))
NT = ((1,), (1,))
TN = ((0,), (0,))


def dot3(a, b, dims):
    return dot(a[0], b[0], dims) + (dot(a[0], b[1], dims) + dot(a[1], b[0], dims))


def recur_kernel(per_step, proj, beta, out, through, total, carry):
    step = pl.program_id(0)

    @pl.when(step == 0)
    def _():
        r = lax.broadcasted_iota(jnp.int32, (2 * DK, DK), 0)
        c = lax.broadcasted_iota(jnp.int32, (2 * DK, DK), 1)
        carry[...] = (r - DK == c).astype(F32)

    row = lax.broadcasted_iota(jnp.int32, (FACTORS, FACTORS), 0)
    col = lax.broadcasted_iota(jnp.int32, (FACTORS, FACTORS), 1)
    row_t, col_t = row & (BLOCK - 1), col & (BLOCK - 1)
    strict = (row_t > col_t) | ((row_t == col_t) & (row > col))
    apart = row_t ^ col_t
    eye = (row == col).astype(F32)
    causal = lax.broadcasted_iota(jnp.int32, (BLOCK, FACTORS), 0) >= (
        lax.broadcasted_iota(jnp.int32, (BLOCK, FACTORS), 1) & (BLOCK - 1))

    blocks = []
    for b in range(per_step):
        rows = slice(b * BLOCK, (b + 1) * BLOCK)
        piece = lambda n: proj[rows, n * DK:(n + 1) * DK]
        query = piece(0)
        keys = jnp.concatenate([piece(1 + j) for j in range(NF)], axis=0).astype(F32)
        vals = jnp.concatenate([piece(1 + NF + j) for j in range(NF)], axis=0).astype(F32)
        betas = jnp.concatenate([beta[rows, j:j + 1] for j in range(NF)], axis=0)
        unit = keys / jnp.sqrt(jnp.sum(keys * keys, axis=-1, keepdims=True) + EPSILON)
        unit = (unit, halves(unit))
        low = jnp.where(strict, betas * dot3(unit[1], unit[1], NT), 0.0)
        scores = jnp.where(causal, dot(query, unit[1][0], NT) + dot(query, unit[1][1], NT), 0.0)
        right = jnp.concatenate([betas * vals, betas * unit[0]], axis=1)
        blocks.append(dict(query=query, unit=unit, low=low, scores=scores, right=right, rows=rows))
    for k in blocks:
        near = jnp.where(apart == 0, k["low"], 0.0)
        parts = halves(near)
        k["inv"] = eye - near + dot3(parts, parts, NN)
    reach = 1
    while reach < BLOCK:
        for k in blocks:
            cross = jnp.where((apart >= reach) & (apart < 2 * reach), k["low"], 0.0)
            inv = halves(k["inv"])
            k["mid"] = halves(dot3(halves(cross), inv, NN))
            k["inv_parts"] = inv
        for k in blocks:
            k["inv"] = k["inv"] - dot3(k["inv_parts"], k["mid"], NN)
        reach *= 2
    for k in blocks:
        k["solved"] = halves(dot3(halves(k["inv"]), halves(k["right"]), NN))
    for k in blocks:
        k["moves"] = dot3(k["solved"], k["unit"][1], TN)
        k["seen"] = dot3(halves(k["scores"]), k["solved"], NN)
    for k in blocks:
        state = carry[...]
        parts = halves(state)
        reader = halves(k["query"].astype(F32) - k["seen"][:, DK:])
        read = dot3(reader, parts, NT)
        out[k["rows"], :] = k["seen"][:, :DK] + read[:, :DK]
        through[k["rows"], :] = read[:, DK:]
        moved = state - dot3(parts, halves(k["moves"][DK:]), NN)
        carry[:DK, :] = moved[:DK] + k["moves"][:DK]
        carry[DK:, :] = moved[DK:]

    @pl.when(step == pl.num_programs(0) - 1)
    def _():
        total[...] = carry[...]


def recur(projected, betas):
    tokens = projected.shape[0]
    per_step = 4
    span = per_step * BLOCK
    return pl.pallas_call(
        functools.partial(recur_kernel, per_step),
        grid=(tokens // span,),
        in_specs=[
            pl.BlockSpec((span, COLS), lambda i: (i, 0)),
            pl.BlockSpec((span, NF), lambda i: (i, 0)),
        ],
        out_specs=(
            pl.BlockSpec((span, DK), lambda i: (i, 0)),
            pl.BlockSpec((span, DK), lambda i: (i, 0)),
            pl.BlockSpec((2 * DK, DK), lambda i: (0, 0)),
        ),
        out_shape=(
            jax.ShapeDtypeStruct((tokens, DK), F32),
            jax.ShapeDtypeStruct((tokens, DK), F32),
            jax.ShapeDtypeStruct((2 * DK, DK), F32),
        ),
        scratch_shapes=[pltpu.VMEM((2 * DK, DK), F32)],
        compiler_params=pltpu.CompilerParams(vmem_limit_bytes=40 * 1024 * 1024),
    )(projected, betas)


def shards(activations, w_in, w_beta, beta_bias, head_gain, w_out):
    ctx_n, head_n = lax.axis_size("ctx"), lax.axis_size("head")
    heads = head_gain.shape[0] // DK
    width = activations.shape[1]
    rows = activations.shape[0]
    place = lax.rem(lax.axis_index("ctx"), heads)
    w_beta = jnp.pad(w_beta, ((0, 0), (0, DK - w_beta.shape[1])))
    w_all, beta_all, acts_all, out_all = gather_all(ctx_n, head_n, heads, w_in, w_beta, activations, w_out)
    acts = acts_all.reshape(-1, width)
    proj_sum = jnp.dot(acts, w_all.reshape(width, COLS), preferred_element_type=F32)
    projected = proj_sum.astype(BF16)
    logits = jnp.dot(acts, beta_all.reshape(width, DK), preferred_element_type=F32)
    logits = lax.dynamic_slice_in_dim(logits, place * NF, NF, 1)
    bias = lax.dynamic_slice_in_dim(beta_bias, place * NF, NF, 0)
    betas = 2.0 / (1.0 + jnp.exp(-(logits + bias)))
    out, through, total = recur(projected, betas)
    made, passing = total[:DK], total[DK:]
    route = [(i, i + heads) for i in range(ctx_n - heads)]
    entering = lax.ppermute(made, "ctx", route)
    for _ in range(ctx_n // heads - 2):
        leaving = jnp.dot(entering, passing, precision=PRECISE) + made
        entering = lax.ppermute(leaving, "ctx", route)
    attended = out + jnp.einsum("td,ed->te", through, entering, precision=PRECISE)
    gain = lax.dynamic_slice_in_dim(head_gain, place * DK, DK, 0)
    scale = 1.0 / jnp.sqrt(jnp.mean(attended * attended, axis=-1, keepdims=True) + EPSILON)
    normed = (attended * scale * gain).astype(BF16)
    got = exchange(head_n, heads, rows, normed)
    weights = out_all.reshape(-1, width)
    summed = jnp.zeros((rows, width), F32)
    group = HEADS_DEV * DK
    for n in range(got.shape[0] // HEADS_DEV):
        left = jnp.concatenate([got[n * HEADS_DEV + i] for i in range(HEADS_DEV)], axis=1)
        term = jnp.dot(left, weights[n * group:(n + 1) * group], preferred_element_type=F32)
        summed = summed + lax.optimization_barrier(term.astype(BF16)).astype(F32)
    return summed.astype(BF16)


def solution(mesh):
    return jax.shard_map(
        shards,
        mesh=mesh,
        in_specs=(
            P(("ctx", "head"), None),
            P("ctx", "head"),
            P("ctx", "head"),
            P("head"),
            P("head"),
            P("head", None),
        ),
        out_specs=P(("ctx", "head"), None),
        check_vma=False,
    )
```

```python
import functools

import jax
import jax.numpy as jnp
from jax import lax
from jax.experimental import pallas as pl
from jax.experimental.pallas import tpu as pltpu
from jax.sharding import PartitionSpec as P

DK = 128
NF = 3
BLOCK = 64
HEADS_DEV = 4
FACTORS = BLOCK * NF
COLS = (1 + 2 * NF) * DK
EPSILON = 1e-06
PRECISE = lax.Precision.HIGHEST
MESH = pl.DeviceIdType.MESH
BF16 = jnp.bfloat16
F32 = jnp.float32


def gather_kernel(ctx_n, head_n, heads, w_in, w_beta, acts, w_out, w_all, beta_all, acts_all, out_all,
                  local_sem, w_send, w_recv, b_send, b_recv, a_send, a_recv, o_send, o_recv):
    ctx, head = lax.axis_index("ctx"), lax.axis_index("head")
    place = lax.rem(ctx, heads)
    base = ctx - place
    pairs = head_n // 2
    core = lax.rem(head, 2)
    pair = head // 2
    sibling = (ctx, pair * 2 + (1 - core))

    def across(dx):
        return (ctx, lax.rem(pair + dx, pairs) * 2 + core)

    def teammate(dc):
        return (base + lax.rem(place + dc, heads), head)

    barrier = pltpu.get_barrier_semaphore()
    for off in range(1, ctx_n):
        pl.semaphore_signal(barrier, inc=1, device_id=(lax.rem(ctx + off, ctx_n), head), device_id_type=MESH)
    for dx in range(1, pairs):
        pl.semaphore_signal(barrier, inc=1, device_id=across(dx), device_id_type=MESH)
    pl.semaphore_signal(barrier, inc=1, device_id=sibling, device_id_type=MESH)
    pl.semaphore_wait(barrier, ctx_n - 1 + pairs)

    def columns(of):
        return w_in.at[:, pl.ds(pl.multiple_of(lax.rem(of, heads) * COLS, DK), COLS)]

    started, finish = [], []

    def send(src, dst, ssem, rsem, device):
        copy = pltpu.make_async_remote_copy(src_ref=src, dst_ref=dst, send_sem=ssem, recv_sem=rsem,
                                            device_id=device, device_id_type=MESH)
        copy.start()
        started.append(copy)
        return copy

    def head_at(dx, dcore):
        return lax.rem(pair + pairs - dx, pairs) * 2 + lax.rem(core + dcore, 2)

    def act_slot(dc, dx, dcore):
        return acts_all.at[lax.rem(place + heads - dc, heads) * head_n + head_at(dx, dcore)]

    def index_of(dc, dx, dcore):
        return (dc * pairs + dx) * 2 + dcore

    def send_acts(src, came, lands, device):
        send(src, act_slot(*came), a_send.at[index_of(*lands)], a_recv.at[index_of(*lands)], device)

    def wait_acts(*came):
        n = index_of(*came)
        pltpu.make_async_remote_copy(src_ref=acts, dst_ref=act_slot(*came), send_sem=a_send.at[n],
                                     recv_sem=a_recv.at[n], device_id=sibling, device_id_type=MESH).wait_recv()

    def send_out(src, came, n, device):
        send(src, out_all.at[head_at(came, 0)], o_send.at[n], o_recv.at[n], device)

    def wait_out(dx, dcore):
        n = dx * 2 + dcore
        pltpu.make_async_remote_copy(src_ref=w_out, dst_ref=out_all.at[head_at(dx, dcore)], send_sem=o_send.at[n],
                                     recv_sem=o_recv.at[n], device_id=sibling, device_id_type=MESH).wait_recv()

    mine = (0, 0, 0)
    for dc in range(1, heads):
        send_acts(acts, mine, (dc, 0, 0), teammate(dc))
    for dx in range(1, pairs):
        send_acts(acts, mine, (0, dx, 0), across(dx))
    send_acts(acts, mine, (0, 0, 1), sibling)
    order = sorted(range(1, ctx_n), key=lambda off: -min(off, ctx_n - off))
    for off in order:
        to = lax.rem(ctx + off, ctx_n)
        finish.append(send(columns(to), w_all.at[ctx], w_send.at[off], w_recv.at[off], (to, head)))
        finish.append(send(w_beta, beta_all.at[ctx], b_send.at[off], b_recv.at[off], (to, head)))
    for dx in range(1, pairs):
        send_out(w_out, 0, dx * 2, across(dx))
    send_out(w_out, 0, 1, sibling)
    own = [
        pltpu.make_async_copy(columns(ctx), w_all.at[ctx], local_sem.at[0]),
        pltpu.make_async_copy(w_beta, beta_all.at[ctx], local_sem.at[1]),
        pltpu.make_async_copy(acts, acts_all.at[place * head_n + head], local_sem.at[2]),
        pltpu.make_async_copy(w_out, out_all.at[head], local_sem.at[3]),
    ]
    for copy in own:
        copy.start()
    for dc in range(1, heads):
        came = (dc, 0, 0)
        wait_acts(*came)
        for dx in range(1, pairs):
            send_acts(act_slot(*came), came, (dc, dx, 0), across(dx))
        send_acts(act_slot(*came), came, (dc, 0, 1), sibling)
    for dc in range(heads):
        for dx in range(1, pairs):
            came = (dc, dx, 0)
            wait_acts(*came)
            send_acts(act_slot(*came), came, (dc, dx, 1), sibling)
    for dx in range(1, pairs):
        wait_out(dx, 0)
        send_out(out_all.at[head_at(dx, 0)], dx, dx * 2 + 1, sibling)
    for dc in range(heads):
        for dx in range(pairs):
            wait_acts(dc, dx, 1)
    for dx in range(pairs):
        wait_out(dx, 1)
    for copy in finish:
        copy.wait_recv()
    for copy in started:
        copy.wait_send()
    for copy in own:
        copy.wait()


def gather_all(ctx_n, head_n, heads, w_in, w_beta, acts, w_out):
    team = heads * head_n
    sems = [pltpu.SemaphoreType.DMA((n,)) for n in (4, ctx_n, ctx_n, ctx_n, ctx_n, team, team, head_n, head_n)]
    return pl.pallas_call(
        functools.partial(gather_kernel, ctx_n, head_n, heads),
        out_shape=(
            jax.ShapeDtypeStruct((ctx_n, w_in.shape[0], COLS), BF16),
            jax.ShapeDtypeStruct((ctx_n,) + w_beta.shape, BF16),
            jax.ShapeDtypeStruct((team,) + acts.shape, BF16),
            jax.ShapeDtypeStruct((head_n,) + w_out.shape, BF16),
        ),
        in_specs=[pl.BlockSpec(memory_space=pl.ANY)] * 4,
        out_specs=(pl.BlockSpec(memory_space=pl.ANY),) * 4,
        scratch_shapes=sems,
        compiler_params=pltpu.CompilerParams(collective_id=0, has_side_effects=True),
    )(w_in, w_beta, acts, w_out)


def exchange_kernel(head_n, heads, rows, mine, weights, mixed, got, held, local_sem, held_sem, send_sem, recv_sem):
    ctx, head = lax.axis_index("ctx"), lax.axis_index("head")
    place = lax.rem(ctx, heads)
    base = ctx - place
    team = [(dc, dg) for dc in range(heads) for dg in range(head_n) if (dc, dg) != (0, 0)]
    fetch = pltpu.make_async_copy(weights, held, held_sem)
    fetch.start()
    barrier = pltpu.get_barrier_semaphore()
    for dc, dg in team:
        device = (base + lax.rem(place + dc, heads), lax.rem(head + dg, head_n))
        pl.semaphore_signal(barrier, inc=1, device_id=device, device_id_type=MESH)
    pl.semaphore_wait(barrier, len(team))
    own_slot = head * heads + place

    def tokens_of(to_place, to_head):
        return mine.at[pl.ds(pl.multiple_of((to_place * head_n + to_head) * rows, rows), rows), :]

    copies = []
    for n, (dc, dg) in enumerate(team):
        to_place, to_head = lax.rem(place + dc, heads), lax.rem(head + dg, head_n)
        copy = pltpu.make_async_remote_copy(
            src_ref=tokens_of(to_place, to_head), dst_ref=got.at[own_slot], send_sem=send_sem.at[n],
            recv_sem=recv_sem.at[n], device_id=(base + to_place, to_head), device_id_type=MESH)
        copy.start()
        copies.append(copy)
    own = pltpu.make_async_copy(tokens_of(place, head), got.at[own_slot], local_sem)
    own.start()
    for copy in [own, fetch] + copies:
        copy.wait()
    group = HEADS_DEV * DK
    lefts = [
        jnp.concatenate([got[n * HEADS_DEV + i] for i in range(HEADS_DEV)], axis=1)
        for n in range(heads * head_n // HEADS_DEV)
    ]
    tile = 512
    for at in range(0, mixed.shape[1], tile):
        summed = None
        for n, left in enumerate(lefts):
            term = jnp.dot(left, held[n * group:(n + 1) * group, at:at + tile], preferred_element_type=F32)
            term = term.astype(BF16).astype(F32)
            summed = term if summed is None else summed + term
        mixed[:, at:at + tile] = summed.astype(BF16)


def exchange(head_n, heads, rows, normed, weights):
    team = heads * head_n
    dma = pltpu.SemaphoreType.DMA
    return pl.pallas_call(
        functools.partial(exchange_kernel, head_n, heads, rows),
        out_shape=jax.ShapeDtypeStruct((rows, weights.shape[1]), BF16),
        in_specs=[pl.BlockSpec(memory_space=pltpu.VMEM), pl.BlockSpec(memory_space=pl.ANY)],
        out_specs=pl.BlockSpec(memory_space=pltpu.VMEM),
        scratch_shapes=[
            pltpu.VMEM((team, rows, DK), BF16),
            pltpu.VMEM(weights.shape, BF16),
            dma, dma, dma((team,)), dma((team,)),
        ],
        compiler_params=pltpu.CompilerParams(collective_id=1, has_side_effects=True, vmem_limit_bytes=40 * 1024 * 1024),
    )(normed, weights)


def halves(x):
    top = x.astype(BF16)
    return top, (x - top.astype(F32)).astype(BF16)


def dot(a, b, dims):
    return lax.dot_general(a, b, (dims, ((), ())), preferred_element_type=F32)


NN = ((1,), (0,))
NT = ((1,), (1,))
TN = ((0,), (0,))


def dot3(a, b, dims):
    return dot(a[0], b[0], dims) + (dot(a[0], b[1], dims) + dot(a[1], b[0], dims))


def recur_kernel(per_step, proj, beta, out, through, total, carry):
    step = pl.program_id(0)

    @pl.when(step == 0)
    def _():
        r = lax.broadcasted_iota(jnp.int32, (2 * DK, DK), 0)
        c = lax.broadcasted_iota(jnp.int32, (2 * DK, DK), 1)
        carry[...] = (r - DK == c).astype(F32)

    row = lax.broadcasted_iota(jnp.int32, (FACTORS, FACTORS), 0)
    col = lax.broadcasted_iota(jnp.int32, (FACTORS, FACTORS), 1)
    row_t, col_t = row & (BLOCK - 1), col & (BLOCK - 1)
    strict = (row_t > col_t) | ((row_t == col_t) & (row > col))
    apart = row_t ^ col_t
    eye = (row == col).astype(F32)
    causal = lax.broadcasted_iota(jnp.int32, (BLOCK, FACTORS), 0) >= (
        lax.broadcasted_iota(jnp.int32, (BLOCK, FACTORS), 1) & (BLOCK - 1))

    blocks = []
    for b in range(per_step):
        rows = slice(b * BLOCK, (b + 1) * BLOCK)
        piece = lambda n: proj[rows, n * DK:(n + 1) * DK]
        query = piece(0)
        keys = jnp.concatenate([piece(1 + j) for j in range(NF)], axis=0).astype(F32)
        vals = jnp.concatenate([piece(1 + NF + j) for j in range(NF)], axis=0).astype(F32)
        betas = jnp.concatenate([beta[rows, j:j + 1] for j in range(NF)], axis=0)
        unit = keys / jnp.sqrt(jnp.sum(keys * keys, axis=-1, keepdims=True) + EPSILON)
        unit = (unit, halves(unit))
        low = jnp.where(strict, betas * dot3(unit[1], unit[1], NT), 0.0)
        scores = jnp.where(causal, dot(query, unit[1][0], NT) + dot(query, unit[1][1], NT), 0.0)
        right = jnp.concatenate([betas * vals, betas * unit[0]], axis=1)
        blocks.append(dict(query=query, unit=unit, low=low, scores=scores, right=right, rows=rows))
    for k in blocks:
        near = jnp.where(apart == 0, k["low"], 0.0)
        parts = halves(near)
        k["inv"] = eye - near + dot3(parts, parts, NN)
    reach = 1
    while reach < BLOCK:
        for k in blocks:
            cross = jnp.where((apart >= reach) & (apart < 2 * reach), k["low"], 0.0)
            inv = halves(k["inv"])
            k["mid"] = halves(dot3(halves(cross), inv, NN))
            k["inv_parts"] = inv
        for k in blocks:
            k["inv"] = k["inv"] - dot3(k["inv_parts"], k["mid"], NN)
        reach *= 2
    for k in blocks:
        k["solved"] = halves(dot3(halves(k["inv"]), halves(k["right"]), NN))
    for k in blocks:
        k["moves"] = dot3(k["solved"], k["unit"][1], TN)
        k["seen"] = dot3(halves(k["scores"]), k["solved"], NN)
    for k in blocks:
        state = carry[...]
        parts = halves(state)
        reader = halves(k["query"].astype(F32) - k["seen"][:, DK:])
        read = dot3(reader, parts, NT)
        out[k["rows"], :] = k["seen"][:, :DK] + read[:, :DK]
        through[k["rows"], :] = read[:, DK:]
        moved = state - dot3(parts, halves(k["moves"][DK:]), NN)
        carry[:DK, :] = moved[:DK] + k["moves"][:DK]
        carry[DK:, :] = moved[DK:]

    @pl.when(step == pl.num_programs(0) - 1)
    def _():
        total[...] = carry[...]


def recur(projected, betas):
    tokens = projected.shape[0]
    per_step = 4
    span = per_step * BLOCK
    return pl.pallas_call(
        functools.partial(recur_kernel, per_step),
        grid=(tokens // span,),
        in_specs=[
            pl.BlockSpec((span, COLS), lambda i: (i, 0)),
            pl.BlockSpec((span, NF), lambda i: (i, 0)),
        ],
        out_specs=(
            pl.BlockSpec((span, DK), lambda i: (i, 0)),
            pl.BlockSpec((span, DK), lambda i: (i, 0)),
            pl.BlockSpec((2 * DK, DK), lambda i: (0, 0)),
        ),
        out_shape=(
            jax.ShapeDtypeStruct((tokens, DK), F32),
            jax.ShapeDtypeStruct((tokens, DK), F32),
            jax.ShapeDtypeStruct((2 * DK, DK), F32),
        ),
        scratch_shapes=[pltpu.VMEM((2 * DK, DK), F32)],
        compiler_params=pltpu.CompilerParams(vmem_limit_bytes=40 * 1024 * 1024),
    )(projected, betas)


def shards(activations, w_in, w_beta, beta_bias, head_gain, w_out):
    ctx_n, head_n = lax.axis_size("ctx"), lax.axis_size("head")
    heads = head_gain.shape[0] // DK
    width = activations.shape[1]
    rows = activations.shape[0]
    place = lax.rem(lax.axis_index("ctx"), heads)
    w_beta = jnp.pad(w_beta, ((0, 0), (0, DK - w_beta.shape[1])))
    w_all, beta_all, acts_all, out_all = gather_all(ctx_n, head_n, heads, w_in, w_beta, activations, w_out)
    acts = acts_all.reshape(-1, width)
    proj_sum = jnp.dot(acts, w_all.reshape(width, COLS), preferred_element_type=F32)
    projected = proj_sum.astype(BF16)
    logits = jnp.dot(acts, beta_all.reshape(width, DK), preferred_element_type=F32)
    logits = lax.dynamic_slice_in_dim(logits, place * NF, NF, 1)
    bias = lax.dynamic_slice_in_dim(beta_bias, place * NF, NF, 0)
    betas = 2.0 / (1.0 + jnp.exp(-(logits + bias)))
    out, through, total = recur(projected, betas)
    made, passing = total[:DK], total[DK:]
    route = [(i, i + heads) for i in range(ctx_n - heads)]
    entering = lax.ppermute(made, "ctx", route)
    for _ in range(ctx_n // heads - 2):
        leaving = jnp.dot(entering, passing, precision=PRECISE) + made
        entering = lax.ppermute(leaving, "ctx", route)
    attended = out + jnp.einsum("td,ed->te", through, entering, precision=PRECISE)
    gain = lax.dynamic_slice_in_dim(head_gain, place * DK, DK, 0)
    scale = 1.0 / jnp.sqrt(jnp.mean(attended * attended, axis=-1, keepdims=True) + EPSILON)
    normed = (attended * scale * gain).astype(BF16)
    return exchange(head_n, heads, rows, normed, out_all.reshape(-1, width))


def solution(mesh):
    return jax.shard_map(
        shards,
        mesh=mesh,
        in_specs=(
            P(("ctx", "head"), None),
            P("ctx", "head"),
            P("ctx", "head"),
            P("head"),
            P("head"),
            P("head", None),
        ),
        out_specs=P(("ctx", "head"), None),
        check_vma=False,
    )
```

```python
import functools

import jax
import jax.numpy as jnp
from jax import lax
from jax.experimental import pallas as pl
from jax.experimental.pallas import tpu as pltpu
from jax.sharding import PartitionSpec as P

DK = 128
NF = 3
BLOCK = 64
HEADS_DEV = 4
FACTORS = BLOCK * NF
COLS = (1 + 2 * NF) * DK
EPSILON = 1e-06
PRECISE = lax.Precision.HIGHEST
MESH = pl.DeviceIdType.MESH
BF16 = jnp.bfloat16
F32 = jnp.float32


def gather_kernel(ctx_n, head_n, heads, w_in, w_beta, acts, w_out, w_all, beta_all, acts_all, out_all,
                  local_sem, w_send, w_recv, b_send, b_recv, a_send, a_recv, o_send, o_recv):
    ctx, head = lax.axis_index("ctx"), lax.axis_index("head")
    place = lax.rem(ctx, heads)
    base = ctx - place
    pairs = head_n // 2
    core = lax.rem(head, 2)
    pair = head // 2
    sibling = (ctx, pair * 2 + (1 - core))

    def across(dx):
        return (ctx, lax.rem(pair + dx, pairs) * 2 + core)

    def teammate(dc):
        return (base + lax.rem(place + dc, heads), head)

    barrier = pltpu.get_barrier_semaphore()
    for off in range(1, ctx_n):
        pl.semaphore_signal(barrier, inc=1, device_id=(lax.rem(ctx + off, ctx_n), head), device_id_type=MESH)
    for dx in range(1, pairs):
        pl.semaphore_signal(barrier, inc=1, device_id=across(dx), device_id_type=MESH)
    pl.semaphore_signal(barrier, inc=1, device_id=sibling, device_id_type=MESH)
    pl.semaphore_wait(barrier, ctx_n - 1 + pairs)

    def columns(of):
        return w_in.at[:, pl.ds(pl.multiple_of(lax.rem(of, heads) * COLS, DK), COLS)]

    started, finish = [], []

    def send(src, dst, ssem, rsem, device):
        copy = pltpu.make_async_remote_copy(src_ref=src, dst_ref=dst, send_sem=ssem, recv_sem=rsem,
                                            device_id=device, device_id_type=MESH)
        copy.start()
        started.append(copy)
        return copy

    def head_at(dx, dcore):
        return lax.rem(pair + pairs - dx, pairs) * 2 + lax.rem(core + dcore, 2)

    def act_slot(dc, dx, dcore):
        return acts_all.at[lax.rem(place + heads - dc, heads) * head_n + head_at(dx, dcore)]

    def index_of(dc, dx, dcore):
        return (dc * pairs + dx) * 2 + dcore

    def send_acts(src, came, lands, device):
        send(src, act_slot(*came), a_send.at[index_of(*lands)], a_recv.at[index_of(*lands)], device)

    def wait_acts(*came):
        n = index_of(*came)
        pltpu.make_async_remote_copy(src_ref=acts, dst_ref=act_slot(*came), send_sem=a_send.at[n],
                                     recv_sem=a_recv.at[n], device_id=sibling, device_id_type=MESH).wait_recv()

    def send_out(src, came, n, device):
        send(src, out_all.at[head_at(came, 0)], o_send.at[n], o_recv.at[n], device)

    def wait_out(dx, dcore):
        n = dx * 2 + dcore
        pltpu.make_async_remote_copy(src_ref=w_out, dst_ref=out_all.at[head_at(dx, dcore)], send_sem=o_send.at[n],
                                     recv_sem=o_recv.at[n], device_id=sibling, device_id_type=MESH).wait_recv()

    mine = (0, 0, 0)
    for dc in range(1, heads):
        send_acts(acts, mine, (dc, 0, 0), teammate(dc))
    for dx in range(1, pairs):
        send_acts(acts, mine, (0, dx, 0), across(dx))
    send_acts(acts, mine, (0, 0, 1), sibling)
    order = sorted(range(1, ctx_n), key=lambda off: -min(off, ctx_n - off))
    for off in order:
        to = lax.rem(ctx + off, ctx_n)
        finish.append(send(columns(to), w_all.at[ctx], w_send.at[off], w_recv.at[off], (to, head)))
        finish.append(send(w_beta, beta_all.at[ctx], b_send.at[off], b_recv.at[off], (to, head)))
    for dx in range(1, pairs):
        send_out(w_out, 0, dx * 2, across(dx))
    send_out(w_out, 0, 1, sibling)
    own = [
        pltpu.make_async_copy(columns(ctx), w_all.at[ctx], local_sem.at[0]),
        pltpu.make_async_copy(w_beta, beta_all.at[ctx], local_sem.at[1]),
        pltpu.make_async_copy(acts, acts_all.at[place * head_n + head], local_sem.at[2]),
        pltpu.make_async_copy(w_out, out_all.at[head], local_sem.at[3]),
    ]
    for copy in own:
        copy.start()
    for dc in range(1, heads):
        came = (dc, 0, 0)
        wait_acts(*came)
        for dx in range(1, pairs):
            send_acts(act_slot(*came), came, (dc, dx, 0), across(dx))
        send_acts(act_slot(*came), came, (dc, 0, 1), sibling)
    for dc in range(heads):
        for dx in range(1, pairs):
            came = (dc, dx, 0)
            wait_acts(*came)
            send_acts(act_slot(*came), came, (dc, dx, 1), sibling)
    for dx in range(1, pairs):
        wait_out(dx, 0)
        send_out(out_all.at[head_at(dx, 0)], dx, dx * 2 + 1, sibling)
    for dc in range(heads):
        for dx in range(pairs):
            wait_acts(dc, dx, 1)
    for dx in range(pairs):
        wait_out(dx, 1)
    for copy in finish:
        copy.wait_recv()
    for copy in started:
        copy.wait_send()
    for copy in own:
        copy.wait()


def gather_all(ctx_n, head_n, heads, w_in, w_beta, acts, w_out):
    team = heads * head_n
    sems = [pltpu.SemaphoreType.DMA((n,)) for n in (4, ctx_n, ctx_n, ctx_n, ctx_n, team, team, head_n, head_n)]
    return pl.pallas_call(
        functools.partial(gather_kernel, ctx_n, head_n, heads),
        out_shape=(
            jax.ShapeDtypeStruct((ctx_n, w_in.shape[0], COLS), BF16),
            jax.ShapeDtypeStruct((ctx_n,) + w_beta.shape, BF16),
            jax.ShapeDtypeStruct((team,) + acts.shape, BF16),
            jax.ShapeDtypeStruct((head_n,) + w_out.shape, BF16),
        ),
        in_specs=[pl.BlockSpec(memory_space=pl.ANY)] * 4,
        out_specs=(pl.BlockSpec(memory_space=pl.ANY),) * 4,
        scratch_shapes=sems,
        compiler_params=pltpu.CompilerParams(collective_id=0, has_side_effects=True),
    )(w_in, w_beta, acts, w_out)


def exchange_kernel(head_n, heads, rows, mine, weights, mixed, got, held, local_sem, held_sem, send_sem, recv_sem):
    ctx, head = lax.axis_index("ctx"), lax.axis_index("head")
    place = lax.rem(ctx, heads)
    base = ctx - place
    team = [(dc, dg) for dc in range(heads) for dg in range(head_n) if (dc, dg) != (0, 0)]
    fetch = pltpu.make_async_copy(weights, held, held_sem)
    fetch.start()
    barrier = pltpu.get_barrier_semaphore()
    for dc, dg in team:
        device = (base + lax.rem(place + dc, heads), lax.rem(head + dg, head_n))
        pl.semaphore_signal(barrier, inc=1, device_id=device, device_id_type=MESH)
    pl.semaphore_wait(barrier, len(team))
    own_slot = head * heads + place

    def tokens_of(to_place, to_head):
        return mine.at[pl.ds(pl.multiple_of((to_place * head_n + to_head) * rows, rows), rows), :]

    copies = []
    for n, (dc, dg) in enumerate(team):
        to_place, to_head = lax.rem(place + dc, heads), lax.rem(head + dg, head_n)
        copy = pltpu.make_async_remote_copy(
            src_ref=tokens_of(to_place, to_head), dst_ref=got.at[own_slot], send_sem=send_sem.at[n],
            recv_sem=recv_sem.at[n], device_id=(base + to_place, to_head), device_id_type=MESH)
        copy.start()
        copies.append(copy)
    own = pltpu.make_async_copy(tokens_of(place, head), got.at[own_slot], local_sem)
    own.start()
    for copy in [own, fetch] + copies:
        copy.wait()
    group = HEADS_DEV * DK
    lefts = [
        jnp.concatenate([got[n * HEADS_DEV + i] for i in range(HEADS_DEV)], axis=1)
        for n in range(heads * head_n // HEADS_DEV)
    ]
    tile = 512
    for at in range(0, mixed.shape[1], tile):
        summed = None
        for n, left in enumerate(lefts):
            term = jnp.dot(left, held[n * group:(n + 1) * group, at:at + tile], preferred_element_type=F32)
            term = term.astype(BF16).astype(F32)
            summed = term if summed is None else summed + term
        mixed[:, at:at + tile] = summed.astype(BF16)


def exchange(head_n, heads, rows, normed, weights):
    team = heads * head_n
    dma = pltpu.SemaphoreType.DMA
    return pl.pallas_call(
        functools.partial(exchange_kernel, head_n, heads, rows),
        out_shape=jax.ShapeDtypeStruct((rows, weights.shape[1]), BF16),
        in_specs=[pl.BlockSpec(memory_space=pltpu.VMEM), pl.BlockSpec(memory_space=pl.ANY)],
        out_specs=pl.BlockSpec(memory_space=pltpu.VMEM),
        scratch_shapes=[
            pltpu.VMEM((team, rows, DK), BF16),
            pltpu.VMEM(weights.shape, BF16),
            dma, dma, dma((team,)), dma((team,)),
        ],
        compiler_params=pltpu.CompilerParams(collective_id=1, has_side_effects=True, vmem_limit_bytes=56 * 1024 * 1024),
    )(normed, weights)


def halves(x):
    top = x.astype(BF16)
    return top, (x - top.astype(F32)).astype(BF16)


def dot(a, b, dims):
    return lax.dot_general(a, b, (dims, ((), ())), preferred_element_type=F32)


NN = ((1,), (0,))
NT = ((1,), (1,))
TN = ((0,), (0,))


def dot3(a, b, dims):
    return dot(a[0], b[0], dims) + (dot(a[0], b[1], dims) + dot(a[1], b[0], dims))


def recur_kernel(per_step, heads, acts, w_head, w_beta, bias, out, through, total, carry):
    step = pl.program_id(0)
    first = lax.rem(lax.axis_index("ctx"), heads) * NF
    proj = jnp.dot(acts[...], w_head[...], preferred_element_type=F32).astype(BF16)
    logits = jnp.dot(acts[...], w_beta[...], preferred_element_type=F32) + bias[...]
    gates = 2.0 / (1.0 + jnp.exp(-logits))
    lane = lax.broadcasted_iota(jnp.int32, gates.shape, 1)
    beta = [jnp.sum(jnp.where(lane == first + j, gates, 0.0), axis=1, keepdims=True) for j in range(NF)]

    @pl.when(step == 0)
    def _():
        r = lax.broadcasted_iota(jnp.int32, (2 * DK, DK), 0)
        c = lax.broadcasted_iota(jnp.int32, (2 * DK, DK), 1)
        carry[...] = (r - DK == c).astype(F32)

    row = lax.broadcasted_iota(jnp.int32, (FACTORS, FACTORS), 0)
    col = lax.broadcasted_iota(jnp.int32, (FACTORS, FACTORS), 1)
    row_t, col_t = row & (BLOCK - 1), col & (BLOCK - 1)
    strict = (row_t > col_t) | ((row_t == col_t) & (row > col))
    apart = row_t ^ col_t
    eye = (row == col).astype(F32)
    causal = lax.broadcasted_iota(jnp.int32, (BLOCK, FACTORS), 0) >= (
        lax.broadcasted_iota(jnp.int32, (BLOCK, FACTORS), 1) & (BLOCK - 1))

    blocks = []
    for b in range(per_step):
        rows = slice(b * BLOCK, (b + 1) * BLOCK)
        piece = lambda n: proj[rows, n * DK:(n + 1) * DK]
        query = piece(0)
        keys = jnp.concatenate([piece(1 + j) for j in range(NF)], axis=0).astype(F32)
        vals = jnp.concatenate([piece(1 + NF + j) for j in range(NF)], axis=0).astype(F32)
        betas = jnp.concatenate([beta[j][rows] for j in range(NF)], axis=0)
        unit = keys / jnp.sqrt(jnp.sum(keys * keys, axis=-1, keepdims=True) + EPSILON)
        unit = (unit, halves(unit))
        low = jnp.where(strict, betas * dot3(unit[1], unit[1], NT), 0.0)
        scores = jnp.where(causal, dot(query, unit[1][0], NT) + dot(query, unit[1][1], NT), 0.0)
        right = jnp.concatenate([betas * vals, betas * unit[0]], axis=1)
        blocks.append(dict(query=query, unit=unit, low=low, scores=scores, right=right, rows=rows))
    for k in blocks:
        near = jnp.where(apart == 0, k["low"], 0.0)
        parts = near.astype(BF16)
        k["inv"] = eye - near + dot(parts, parts, NN)
    reach = 1
    while reach < BLOCK:
        for k in blocks:
            cross = jnp.where((apart >= reach) & (apart < 2 * reach), k["low"], 0.0).astype(BF16)
            k["inv_parts"] = k["inv"].astype(BF16)
            k["mid"] = dot(cross, k["inv_parts"], NN).astype(BF16)
        for k in blocks:
            k["inv"] = k["inv"] - dot(k["inv_parts"], k["mid"], NN)
        reach *= 2
    for k in blocks:
        k["low_parts"] = halves(k["low"])
        k["rough"] = k["inv"].astype(BF16)
    for k in blocks:
        rough = k["rough"]
        left = (eye - rough.astype(F32)) - (dot(k["low_parts"][0], rough, NN) + dot(k["low_parts"][1], rough, NN))
        k["left"] = left.astype(BF16)
    for k in blocks:
        k["inv"] = k["rough"].astype(F32) + dot(k["rough"], k["left"], NN)
    for k in blocks:
        left = (eye - k["inv"]) - dot3(k["low_parts"], halves(k["inv"]), NN)
        k["inv"] = k["inv"] + dot(k["rough"], left.astype(BF16), NN)
    for k in blocks:
        k["solved"] = halves(dot3(halves(k["inv"]), halves(k["right"]), NN))
    for k in blocks:
        k["moves"] = dot3(k["solved"], k["unit"][1], TN)
        k["seen"] = dot3(halves(k["scores"]), k["solved"], NN)
    for k in blocks:
        state = carry[...]
        parts = halves(state)
        reader = halves(k["query"].astype(F32) - k["seen"][:, DK:])
        read = dot3(reader, parts, NT)
        out[k["rows"], :] = k["seen"][:, :DK] + read[:, :DK]
        through[k["rows"], :] = read[:, DK:]
        moved = state - dot3(parts, halves(k["moves"][DK:]), NN)
        carry[:DK, :] = moved[:DK] + k["moves"][:DK]
        carry[DK:, :] = moved[DK:]

    @pl.when(step == pl.num_programs(0) - 1)
    def _():
        total[...] = carry[...]


def recur(heads, acts, w_head, w_beta, bias):
    tokens, width = acts.shape
    per_step = 8
    span = per_step * BLOCK
    return pl.pallas_call(
        functools.partial(recur_kernel, per_step, heads),
        grid=(tokens // span,),
        in_specs=[
            pl.BlockSpec((span, width), lambda i: (i, 0)),
            pl.BlockSpec((width, COLS), lambda i: (0, 0)),
            pl.BlockSpec((width, DK), lambda i: (0, 0)),
            pl.BlockSpec((1, DK), lambda i: (0, 0)),
        ],
        out_specs=(
            pl.BlockSpec((span, DK), lambda i: (i, 0)),
            pl.BlockSpec((span, DK), lambda i: (i, 0)),
            pl.BlockSpec((2 * DK, DK), lambda i: (0, 0)),
        ),
        out_shape=(
            jax.ShapeDtypeStruct((tokens, DK), F32),
            jax.ShapeDtypeStruct((tokens, DK), F32),
            jax.ShapeDtypeStruct((2 * DK, DK), F32),
        ),
        scratch_shapes=[pltpu.VMEM((2 * DK, DK), F32)],
        compiler_params=pltpu.CompilerParams(vmem_limit_bytes=56 * 1024 * 1024),
    )(acts, w_head, w_beta, bias)


def shards(activations, w_in, w_beta, beta_bias, head_gain, w_out):
    ctx_n, head_n = lax.axis_size("ctx"), lax.axis_size("head")
    heads = head_gain.shape[0] // DK
    width = activations.shape[1]
    rows = activations.shape[0]
    place = lax.rem(lax.axis_index("ctx"), heads)
    w_beta = jnp.pad(w_beta, ((0, 0), (0, DK - w_beta.shape[1])))
    w_all, beta_all, acts_all, out_all = gather_all(ctx_n, head_n, heads, w_in, w_beta, activations, w_out)
    acts = acts_all.reshape(-1, width)
    bias = jnp.pad(beta_bias, (0, DK - beta_bias.shape[0])).reshape(1, DK)
    out, through, total = recur(heads, acts, w_all.reshape(width, COLS), beta_all.reshape(width, DK), bias)
    made, passing = total[:DK], total[DK:]
    route = [(i, i + heads) for i in range(ctx_n - heads)]
    entering = lax.ppermute(made, "ctx", route)
    for _ in range(ctx_n // heads - 2):
        leaving = jnp.dot(entering, passing, precision=PRECISE) + made
        entering = lax.ppermute(leaving, "ctx", route)
    attended = out + jnp.einsum("td,ed->te", through, entering, precision=PRECISE)
    gain = lax.dynamic_slice_in_dim(head_gain, place * DK, DK, 0)
    scale = 1.0 / jnp.sqrt(jnp.mean(attended * attended, axis=-1, keepdims=True) + EPSILON)
    normed = (attended * scale * gain).astype(BF16)
    return exchange(head_n, heads, rows, normed, out_all.reshape(-1, width))


def solution(mesh):
    return jax.shard_map(
        shards,
        mesh=mesh,
        in_specs=(
            P(("ctx", "head"), None),
            P("ctx", "head"),
            P("ctx", "head"),
            P("head"),
            P("head"),
            P("head", None),
        ),
        out_specs=P(("ctx", "head"), None),
        check_vma=False,
    )
```

```python
import functools

import jax
import jax.numpy as jnp
from jax import lax
from jax.experimental import pallas as pl
from jax.experimental.pallas import tpu as pltpu
from jax.sharding import PartitionSpec as P

DK = 128
NF = 3
BLOCK = 64
HEADS_DEV = 4
FACTORS = BLOCK * NF
COLS = (1 + 2 * NF) * DK
EPSILON = 1e-06
PRECISE = lax.Precision.HIGHEST
MESH = pl.DeviceIdType.MESH
BF16 = jnp.bfloat16
F32 = jnp.float32


def gather_kernel(ctx_n, head_n, heads, w_in, w_beta, acts, w_out, w_all, beta_all, acts_all, out_all,
                  local_sem, w_send, w_recv, b_send, b_recv, a_send, a_recv, o_send, o_recv):
    ctx, head = lax.axis_index("ctx"), lax.axis_index("head")
    place = lax.rem(ctx, heads)
    base = ctx - place
    pairs = head_n // 2
    core = lax.rem(head, 2)
    pair = head // 2
    sibling = (ctx, pair * 2 + (1 - core))

    def across(dx):
        return (ctx, lax.rem(pair + dx, pairs) * 2 + core)

    def teammate(dc):
        return (base + lax.rem(place + dc, heads), head)

    barrier = pltpu.get_barrier_semaphore()
    for off in range(1, ctx_n):
        pl.semaphore_signal(barrier, inc=1, device_id=(lax.rem(ctx + off, ctx_n), head), device_id_type=MESH)
    for dx in range(1, pairs):
        pl.semaphore_signal(barrier, inc=1, device_id=across(dx), device_id_type=MESH)
    pl.semaphore_signal(barrier, inc=1, device_id=sibling, device_id_type=MESH)
    pl.semaphore_wait(barrier, ctx_n - 1 + pairs)

    def columns(of):
        return w_in.at[:, pl.ds(pl.multiple_of(lax.rem(of, heads) * COLS, DK), COLS)]

    started, finish = [], []

    def send(src, dst, ssem, rsem, device):
        copy = pltpu.make_async_remote_copy(src_ref=src, dst_ref=dst, send_sem=ssem, recv_sem=rsem,
                                            device_id=device, device_id_type=MESH)
        copy.start()
        started.append(copy)
        return copy

    def head_at(dx, dcore):
        return lax.rem(pair + pairs - dx, pairs) * 2 + lax.rem(core + dcore, 2)

    def act_slot(dc, dx, dcore):
        return acts_all.at[lax.rem(place + heads - dc, heads) * head_n + head_at(dx, dcore)]

    def index_of(dc, dx, dcore):
        return (dc * pairs + dx) * 2 + dcore

    def send_acts(src, came, lands, device):
        send(src, act_slot(*came), a_send.at[index_of(*lands)], a_recv.at[index_of(*lands)], device)

    def wait_acts(*came):
        n = index_of(*came)
        pltpu.make_async_remote_copy(src_ref=acts, dst_ref=act_slot(*came), send_sem=a_send.at[n],
                                     recv_sem=a_recv.at[n], device_id=sibling, device_id_type=MESH).wait_recv()

    def send_out(src, came, n, device):
        send(src, out_all.at[head_at(came, 0)], o_send.at[n], o_recv.at[n], device)

    def wait_out(dx, dcore):
        n = dx * 2 + dcore
        pltpu.make_async_remote_copy(src_ref=w_out, dst_ref=out_all.at[head_at(dx, dcore)], send_sem=o_send.at[n],
                                     recv_sem=o_recv.at[n], device_id=sibling, device_id_type=MESH).wait_recv()

    mine = (0, 0, 0)
    for dc in range(1, heads):
        send_acts(acts, mine, (dc, 0, 0), teammate(dc))
    for dx in range(1, pairs):
        send_acts(acts, mine, (0, dx, 0), across(dx))
    send_acts(acts, mine, (0, 0, 1), sibling)
    order = sorted(range(1, ctx_n), key=lambda off: -min(off, ctx_n - off))
    for off in order:
        to = lax.rem(ctx + off, ctx_n)
        finish.append(send(columns(to), w_all.at[ctx], w_send.at[off], w_recv.at[off], (to, head)))
        finish.append(send(w_beta, beta_all.at[ctx], b_send.at[off], b_recv.at[off], (to, head)))
    for dx in range(1, pairs):
        send_out(w_out, 0, dx * 2, across(dx))
    send_out(w_out, 0, 1, sibling)
    own = [
        pltpu.make_async_copy(columns(ctx), w_all.at[ctx], local_sem.at[0]),
        pltpu.make_async_copy(w_beta, beta_all.at[ctx], local_sem.at[1]),
        pltpu.make_async_copy(acts, acts_all.at[place * head_n + head], local_sem.at[2]),
        pltpu.make_async_copy(w_out, out_all.at[head], local_sem.at[3]),
    ]
    for copy in own:
        copy.start()
    for dc in range(1, heads):
        came = (dc, 0, 0)
        wait_acts(*came)
        for dx in range(1, pairs):
            send_acts(act_slot(*came), came, (dc, dx, 0), across(dx))
        send_acts(act_slot(*came), came, (dc, 0, 1), sibling)
    for dc in range(heads):
        for dx in range(1, pairs):
            came = (dc, dx, 0)
            wait_acts(*came)
            send_acts(act_slot(*came), came, (dc, dx, 1), sibling)
    for dx in range(1, pairs):
        wait_out(dx, 0)
        send_out(out_all.at[head_at(dx, 0)], dx, dx * 2 + 1, sibling)
    for dc in range(heads):
        for dx in range(pairs):
            wait_acts(dc, dx, 1)
    for dx in range(pairs):
        wait_out(dx, 1)
    for copy in finish:
        copy.wait_recv()
    for copy in started:
        copy.wait_send()
    for copy in own:
        copy.wait()


def gather_all(ctx_n, head_n, heads, w_in, w_beta, acts, w_out):
    team = heads * head_n
    sems = [pltpu.SemaphoreType.DMA((n,)) for n in (4, ctx_n, ctx_n, ctx_n, ctx_n, team, team, head_n, head_n)]
    return pl.pallas_call(
        functools.partial(gather_kernel, ctx_n, head_n, heads),
        out_shape=(
            jax.ShapeDtypeStruct((ctx_n, w_in.shape[0], COLS), BF16),
            jax.ShapeDtypeStruct((ctx_n,) + w_beta.shape, BF16),
            jax.ShapeDtypeStruct((team,) + acts.shape, BF16),
            jax.ShapeDtypeStruct((head_n,) + w_out.shape, BF16),
        ),
        in_specs=[pl.BlockSpec(memory_space=pl.ANY)] * 4,
        out_specs=(pl.BlockSpec(memory_space=pl.ANY),) * 4,
        scratch_shapes=sems,
        compiler_params=pltpu.CompilerParams(collective_id=0, has_side_effects=True),
    )(w_in, w_beta, acts, w_out)


def exchange_kernel(head_n, heads, rows, mine, weights, mixed, got, held, local_sem, held_sem, send_sem, recv_sem):
    ctx, head = lax.axis_index("ctx"), lax.axis_index("head")
    place = lax.rem(ctx, heads)
    base = ctx - place
    team = [(dc, dg) for dc in range(heads) for dg in range(head_n) if (dc, dg) != (0, 0)]
    fetch = pltpu.make_async_copy(weights, held, held_sem)
    fetch.start()
    barrier = pltpu.get_barrier_semaphore()
    for dc, dg in team:
        device = (base + lax.rem(place + dc, heads), lax.rem(head + dg, head_n))
        pl.semaphore_signal(barrier, inc=1, device_id=device, device_id_type=MESH)
    pl.semaphore_wait(barrier, len(team))
    own_slot = head * heads + place

    def tokens_of(to_place, to_head):
        return mine.at[pl.ds(pl.multiple_of((to_place * head_n + to_head) * rows, rows), rows), :]

    copies = []
    for n, (dc, dg) in enumerate(team):
        to_place, to_head = lax.rem(place + dc, heads), lax.rem(head + dg, head_n)
        copy = pltpu.make_async_remote_copy(
            src_ref=tokens_of(to_place, to_head), dst_ref=got.at[own_slot], send_sem=send_sem.at[n],
            recv_sem=recv_sem.at[n], device_id=(base + to_place, to_head), device_id_type=MESH)
        copy.start()
        copies.append(copy)
    own = pltpu.make_async_copy(tokens_of(place, head), got.at[own_slot], local_sem)
    own.start()
    for copy in [own, fetch] + copies:
        copy.wait()
    group = HEADS_DEV * DK
    lefts = [
        jnp.concatenate([got[n * HEADS_DEV + i] for i in range(HEADS_DEV)], axis=1)
        for n in range(heads * head_n // HEADS_DEV)
    ]
    tile = 512
    for at in range(0, mixed.shape[1], tile):
        summed = None
        for n, left in enumerate(lefts):
            term = jnp.dot(left, held[n * group:(n + 1) * group, at:at + tile], preferred_element_type=F32)
            term = term.astype(BF16).astype(F32)
            summed = term if summed is None else summed + term
        mixed[:, at:at + tile] = summed.astype(BF16)


def exchange(head_n, heads, rows, normed, weights):
    team = heads * head_n
    dma = pltpu.SemaphoreType.DMA
    return pl.pallas_call(
        functools.partial(exchange_kernel, head_n, heads, rows),
        out_shape=jax.ShapeDtypeStruct((rows, weights.shape[1]), BF16),
        in_specs=[pl.BlockSpec(memory_space=pltpu.VMEM), pl.BlockSpec(memory_space=pl.ANY)],
        out_specs=pl.BlockSpec(memory_space=pltpu.VMEM),
        scratch_shapes=[
            pltpu.VMEM((team, rows, DK), BF16),
            pltpu.VMEM(weights.shape, BF16),
            dma, dma, dma((team,)), dma((team,)),
        ],
        compiler_params=pltpu.CompilerParams(collective_id=1, has_side_effects=True, vmem_limit_bytes=56 * 1024 * 1024),
    )(normed, weights)


def halves(x):
    top = x.astype(BF16)
    return top, (x - top.astype(F32)).astype(BF16)


def dot(a, b, dims):
    return lax.dot_general(a, b, (dims, ((), ())), preferred_element_type=F32)


NN = ((1,), (0,))
NT = ((1,), (1,))
TN = ((0,), (0,))


def dot3(a, b, dims):
    return dot(a[0], b[0], dims) + (dot(a[0], b[1], dims) + dot(a[1], b[0], dims))


def recur_kernel(per_step, heads, acts, w_head, w_beta, bias, out, through, total, carry):
    step = pl.program_id(0)
    first = lax.rem(lax.axis_index("ctx"), heads) * NF
    proj = jnp.dot(acts[...], w_head[...], preferred_element_type=F32).astype(BF16)
    logits = jnp.dot(acts[...], w_beta[...], preferred_element_type=F32) + bias[...]
    gates = 2.0 / (1.0 + jnp.exp(-logits))
    lane = lax.broadcasted_iota(jnp.int32, gates.shape, 1)
    beta = [jnp.sum(jnp.where(lane == first + j, gates, 0.0), axis=1, keepdims=True) for j in range(NF)]

    @pl.when(step == 0)
    def _():
        r = lax.broadcasted_iota(jnp.int32, (2 * DK, DK), 0)
        c = lax.broadcasted_iota(jnp.int32, (2 * DK, DK), 1)
        carry[...] = (r - DK == c).astype(F32)

    row = lax.broadcasted_iota(jnp.int32, (FACTORS, FACTORS), 0)
    col = lax.broadcasted_iota(jnp.int32, (FACTORS, FACTORS), 1)
    row_t, col_t = row & (BLOCK - 1), col & (BLOCK - 1)
    strict = (row_t > col_t) | ((row_t == col_t) & (row > col))
    apart = row_t ^ col_t
    eye = (row == col).astype(F32)
    causal = lax.broadcasted_iota(jnp.int32, (BLOCK, FACTORS), 0) >= (
        lax.broadcasted_iota(jnp.int32, (BLOCK, FACTORS), 1) & (BLOCK - 1))

    blocks = []
    for b in range(per_step):
        rows = slice(b * BLOCK, (b + 1) * BLOCK)
        piece = lambda n: proj[rows, n * DK:(n + 1) * DK]
        query = piece(0)
        keys = jnp.concatenate([piece(1 + j) for j in range(NF)], axis=0).astype(F32)
        vals = jnp.concatenate([piece(1 + NF + j) for j in range(NF)], axis=0).astype(F32)
        betas = jnp.concatenate([beta[j][rows] for j in range(NF)], axis=0)
        unit = keys / jnp.sqrt(jnp.sum(keys * keys, axis=-1, keepdims=True) + EPSILON)
        unit = (unit, halves(unit))
        low = jnp.where(strict, betas * dot3(unit[1], unit[1], NT), 0.0)
        scores = jnp.where(causal, dot(query, unit[1][0], NT) + dot(query, unit[1][1], NT), 0.0)
        right = jnp.concatenate([betas * vals, betas * unit[0]], axis=1)
        blocks.append(dict(query=query, unit=unit, low=low, scores=scores, right=right, rows=rows))
    for k in blocks:
        near = jnp.where(apart == 0, k["low"], 0.0)
        parts = near.astype(BF16)
        k["inv"] = eye - near + dot(parts, parts, NN)
    reach = 1
    while reach < BLOCK:
        for k in blocks:
            cross = jnp.where((apart >= reach) & (apart < 2 * reach), k["low"], 0.0).astype(BF16)
            k["inv_parts"] = k["inv"].astype(BF16)
            k["mid"] = dot(cross, k["inv_parts"], NN).astype(BF16)
        for k in blocks:
            k["inv"] = k["inv"] - dot(k["inv_parts"], k["mid"], NN)
        reach *= 2
    for k in blocks:
        k["low_parts"] = halves(k["low"])
        k["rough"] = k["inv"].astype(BF16)
    for k in blocks:
        rough = k["rough"]
        left = (eye - rough.astype(F32)) - (dot(k["low_parts"][0], rough, NN) + dot(k["low_parts"][1], rough, NN))
        near = left.astype(BF16)
        k["left"] = halves(left + dot(near, near, NN))
    for k in blocks:
        k["inv"] = k["rough"].astype(F32) + (dot(k["rough"], k["left"][0], NN) + dot(k["rough"], k["left"][1], NN))
    for k in blocks:
        k["solved"] = halves(dot3(halves(k["inv"]), halves(k["right"]), NN))
    for k in blocks:
        k["moves"] = dot3(k["solved"], k["unit"][1], TN)
        k["seen"] = dot3(halves(k["scores"]), k["solved"], NN)
    for k in blocks:
        state = carry[...]
        parts = halves(state)
        reader = halves(k["query"].astype(F32) - k["seen"][:, DK:])
        read = dot3(reader, parts, NT)
        out[k["rows"], :] = k["seen"][:, :DK] + read[:, :DK]
        through[k["rows"], :] = read[:, DK:]
        moved = state - dot3(parts, halves(k["moves"][DK:]), NN)
        carry[:DK, :] = moved[:DK] + k["moves"][:DK]
        carry[DK:, :] = moved[DK:]

    @pl.when(step == pl.num_programs(0) - 1)
    def _():
        total[...] = carry[...]


def recur(heads, acts, w_head, w_beta, bias):
    tokens, width = acts.shape
    per_step = 8
    span = per_step * BLOCK
    return pl.pallas_call(
        functools.partial(recur_kernel, per_step, heads),
        grid=(tokens // span,),
        in_specs=[
            pl.BlockSpec((span, width), lambda i: (i, 0)),
            pl.BlockSpec((width, COLS), lambda i: (0, 0)),
            pl.BlockSpec((width, DK), lambda i: (0, 0)),
            pl.BlockSpec((1, DK), lambda i: (0, 0)),
        ],
        out_specs=(
            pl.BlockSpec((span, DK), lambda i: (i, 0)),
            pl.BlockSpec((span, DK), lambda i: (i, 0)),
            pl.BlockSpec((2 * DK, DK), lambda i: (0, 0)),
        ),
        out_shape=(
            jax.ShapeDtypeStruct((tokens, DK), F32),
            jax.ShapeDtypeStruct((tokens, DK), F32),
            jax.ShapeDtypeStruct((2 * DK, DK), F32),
        ),
        scratch_shapes=[pltpu.VMEM((2 * DK, DK), F32)],
        compiler_params=pltpu.CompilerParams(vmem_limit_bytes=56 * 1024 * 1024),
    )(acts, w_head, w_beta, bias)


def shards(activations, w_in, w_beta, beta_bias, head_gain, w_out):
    ctx_n, head_n = lax.axis_size("ctx"), lax.axis_size("head")
    heads = head_gain.shape[0] // DK
    width = activations.shape[1]
    rows = activations.shape[0]
    place = lax.rem(lax.axis_index("ctx"), heads)
    w_beta = jnp.pad(w_beta, ((0, 0), (0, DK - w_beta.shape[1])))
    w_all, beta_all, acts_all, out_all = gather_all(ctx_n, head_n, heads, w_in, w_beta, activations, w_out)
    acts = acts_all.reshape(-1, width)
    bias = jnp.pad(beta_bias, (0, DK - beta_bias.shape[0])).reshape(1, DK)
    out, through, total = recur(heads, acts, w_all.reshape(width, COLS), beta_all.reshape(width, DK), bias)
    made, passing = total[:DK], total[DK:]
    route = [(i, i + heads) for i in range(ctx_n - heads)]
    entering = lax.ppermute(made, "ctx", route)
    for _ in range(ctx_n // heads - 2):
        leaving = jnp.dot(entering, passing, precision=PRECISE) + made
        entering = lax.ppermute(leaving, "ctx", route)
    attended = out + jnp.einsum("td,ed->te", through, entering, precision=PRECISE)
    gain = lax.dynamic_slice_in_dim(head_gain, place * DK, DK, 0)
    scale = 1.0 / jnp.sqrt(jnp.mean(attended * attended, axis=-1, keepdims=True) + EPSILON)
    normed = (attended * scale * gain).astype(BF16)
    return exchange(head_n, heads, rows, normed, out_all.reshape(-1, width))


def solution(mesh):
    return jax.shard_map(
        shards,
        mesh=mesh,
        in_specs=(
            P(("ctx", "head"), None),
            P("ctx", "head"),
            P("ctx", "head"),
            P("head"),
            P("head"),
            P("head", None),
        ),
        out_specs=P(("ctx", "head"), None),
        check_vma=False,
    )
```
